32 devices in a mesh: expo: 4 (over z), sky: 8 (over y, x, core).
Axes of the slice: x: 2, y: 2, z: 4, core: 2. Of those that a mesh axis runs over, the one named last changes fastest.
Arguments:
- samples: bfloat16 [512, 32, 256], P('sky'), may hold values from -0.75 to 0.75
- basis: bfloat16 [256, 1024], replicated, may hold values from -3 to 3
- operators: bfloat16 [256, 1024, 1024], P(('expo', 'sky')), may hold values from -0.1875 to 0.1875
- cutouts: float32 [256, 16, 1024], P(('expo', 'sky')), may hold values from -6 to 6
- pixel_weights: float32 [256, 16, 1024], P(('expo', 'sky')), may hold values from 0.25 to 4
- detections: int32 [4, 8, 8, 24], P('expo', 'sky'), may hold values from -1 to 63, as said below
- intersections: int32 [256, 16], P(('expo', 'sky')), may hold values from -1 to 191, as said below
Outputs:
- loglik: float32 [512, 32], P('sky', 'expo')
- coeff_grads: float32 [512, 32, 256], P('sky', 'expo')
The draws below stay inside these ranges and needn't reach their ends.
Inputs may be any that keep to these rules, and one draw needn't show every extreme that they name: In detections[e, s, c], the live slots (values 0 or more) come first; -1 marks the rest. For every device (e, c), the live slots over all s total exactly 96, and one s fills all 24. A galaxy may stand in several slots. `intersections`: on device (e, c), a slot r = s * 24 + j is live exactly when detections[e, s, c, j] >= 0, and each live slot stands at exactly one position of the device's tiles; -1 marks empty positions. One tile of every device has all 16 positions filled.
All inputs are finite; a program needn't handle non-finite values.
Results may differ from the reference program's by a relative error of at most 0.0017.
Values may be sent and summed in bfloat16 or wider, within the bound.
A program may use at most 128 MiB of HBM per device.

```python
import math
import jax
import jax.numpy as jnp
from jax import lax

K = 256
P_SIZE = 1024
S = 32
G_DEV = 64
PAIR_DEV = 96
TILE_DEV = 8
TCAP = 16
CAP = 24
GAL = 512
TILES = 256
N_EXPO = 4
N_SKY = 8


def plan_device(key):
    keys = jax.random.split(key, 6)
    full_source = jax.random.randint(keys[0], (), 0, N_SKY)
    chosen = jax.random.permutation(keys[1], (N_SKY - 1) * CAP) < PAIR_DEV - CAP
    other_counts = jnp.sum(chosen.reshape(N_SKY - 1, CAP).astype(jnp.int32), axis=1)
    sources = jnp.arange(N_SKY, dtype=jnp.int32)
    pick = jnp.clip(sources - (sources > full_source).astype(jnp.int32), 0, N_SKY - 2)
    counts = jnp.where(sources == full_source, CAP, other_counts[pick])
    live = jnp.arange(CAP, dtype=jnp.int32)[None, :] < counts[:, None]
    galaxy = jax.random.randint(keys[2], (N_SKY, CAP), 0, G_DEV)
    listed = jnp.where(live, galaxy, -1).astype(jnp.int32)
    full_tile = jax.random.randint(keys[3], (), 0, TILE_DEV)
    filled_other = jax.random.permutation(keys[4], (TILE_DEV - 1) * TCAP) < PAIR_DEV - TCAP
    tile_numbers = jnp.arange(TILE_DEV, dtype=jnp.int32)
    tile_pick = jnp.clip(tile_numbers - (tile_numbers > full_tile).astype(jnp.int32), 0, TILE_DEV - 2)
    filled = jnp.where((tile_numbers == full_tile)[:, None], True, filled_other.reshape(TILE_DEV - 1, TCAP)[tile_pick])
    slot_numbers = jnp.arange(N_SKY * CAP, dtype=jnp.int32)
    order = jnp.argsort(jnp.where(live.reshape(-1), slot_numbers, slot_numbers + N_SKY * CAP), stable=True)[:PAIR_DEV]
    order = order[jax.random.permutation(keys[5], PAIR_DEV)]
    position_numbers = jnp.arange(TILE_DEV * TCAP, dtype=jnp.int32)
    position_order = jnp.argsort(jnp.where(filled.reshape(-1), position_numbers, position_numbers + TILE_DEV * TCAP), stable=True)[:PAIR_DEV]
    placed = jnp.full((TILE_DEV * TCAP,), -1, jnp.int32).at[position_order].set(order.astype(jnp.int32))
    return (listed, placed.reshape(TILE_DEV, TCAP))


def plan_all(key):
    keys = jax.random.split(jax.random.fold_in(key, 11), N_EXPO * N_SKY)
    return jax.vmap(plan_device)(keys)


def draw_detections(key, part):
    listed, placed = plan_all(key)
    return listed.reshape(N_EXPO, N_SKY, N_SKY, CAP).transpose(0, 2, 1, 3)


def draw_intersections(key, part):
    listed, placed = plan_all(key)
    return placed.reshape(TILES, TCAP)


def shard_levels(rng, dims, pieces, least, top_value):
    level = 1.0
    for dim, blocks in pieces:
        heights = jax.random.uniform(jax.random.fold_in(jax.random.fold_in(rng, 6), dim), (blocks,), jnp.float32, least / len(pieces), top_value / len(pieces))
        level = level * jnp.repeat(jnp.exp(heights), dims[dim] // blocks).reshape((-1,) + (1,) * (len(dims) - 1 - dim))
    return level


def noise(rng, extent, width, limit, pieces=(), kind=jnp.bfloat16):
    loudness = shard_levels(rng, extent, pieces, -0.22, 0.18) if pieces else 1.0
    values = jax.random.normal(rng, extent, jnp.float32) * width * loudness
    return jnp.minimum(jnp.maximum(values, -limit), limit).astype(kind)


def setup_inputs(seed: int = 0) -> dict:
    streams_of = jax.random.split(jax.random.key(seed), 8)
    return {
        "samples": noise(streams_of[0], (GAL, S, K), 0.125, 0.75, ((0, 8),)),
        "basis": noise(streams_of[1], (K, P_SIZE), 0.5, 3.0),
        "operators": noise(streams_of[2], (TILES, P_SIZE, P_SIZE), P_SIZE ** -0.5, 0.1875, ((0, 32),)),
        "cutouts": noise(streams_of[3], (TILES, TCAP, P_SIZE), 1.0, 6.0, ((0, 32),), jnp.float32),
        "pixel_weights": jnp.clip(jnp.exp(math.log(4.0) - 2.7725887 * jax.random.uniform(streams_of[4], (TILES, TCAP, P_SIZE), jnp.float32) ** shard_levels(streams_of[4], (TILES, TCAP, P_SIZE), ((0, 32),), -0.2, 0.2)), 0.25, 4.0),
        "detections": draw_detections(jax.random.fold_in(streams_of[7], 71), 0),
        "intersections": draw_intersections(jax.random.fold_in(streams_of[7], 71), 0),
    }


def reference(samples, basis, operators, cutouts, pixel_weights, detections, intersections):
    flat_samples = samples.reshape(GAL, S * K)
    basis_f = basis.astype(jnp.float32)

    def device_step(carry, device):
        grad_acc, like_acc = carry
        row = device // N_SKY
        column = device % N_SKY
        tile_ops = lax.dynamic_slice_in_dim(operators, device * TILE_DEV, TILE_DEV, 0).astype(jnp.float32)
        tile_data = lax.dynamic_slice_in_dim(cutouts, device * TILE_DEV, TILE_DEV, 0)
        tile_weights = lax.dynamic_slice_in_dim(pixel_weights, device * TILE_DEV, TILE_DEV, 0)
        listed = lax.dynamic_slice_in_dim(intersections, device * TILE_DEV, TILE_DEV, 0)
        live = listed >= 0
        slot = jnp.maximum(listed, 0)
        source = slot // CAP
        within = slot % CAP
        local_gal = detections[row, source, column, within]
        galaxy = source * G_DEV + local_gal
        picked = flat_samples[jnp.where(live, galaxy, 0)].reshape(-1, K)
        rendered = jnp.dot(picked, basis, preferred_element_type=jnp.float32).astype(jnp.bfloat16)
        rendered = rendered.reshape(TILE_DEV, TCAP * S, P_SIZE).astype(jnp.float32)
        model = jnp.einsum("tnp,tpq->tnq", rendered, tile_ops).reshape(TILE_DEV, TCAP, S, P_SIZE)
        resid = model - tile_data[:, :, None, :]
        weighted = tile_weights[:, :, None, :] * resid
        pair_like = (-0.5 / P_SIZE) * jnp.sum(weighted * resid, axis=-1)
        scaled = weighted.astype(jnp.bfloat16).reshape(TILE_DEV, TCAP * S, P_SIZE).astype(jnp.float32)
        backed = jnp.einsum("tnq,tpq->tnp", scaled, tile_ops).astype(jnp.bfloat16).astype(jnp.float32)
        pair_grad = (-1.0 / P_SIZE) * jnp.einsum("np,kp->nk", backed.reshape(-1, P_SIZE), basis_f)
        target = jnp.where(live, galaxy, GAL).reshape(-1)
        grad_acc = grad_acc.at[target].add(pair_grad.reshape(TILE_DEV * TCAP, S * K), mode="drop")
        like_acc = like_acc.at[target].add(pair_like.reshape(TILE_DEV * TCAP, S), mode="drop")
        return (grad_acc, like_acc), None

    start = (jnp.zeros((GAL, S * K), jnp.float32), jnp.zeros((GAL, S), jnp.float32))
    (grad_acc, like_acc), _ = lax.scan(device_step, start, jnp.arange(N_EXPO * N_SKY, dtype=jnp.int32))
    return (like_acc, grad_acc.reshape(GAL, S, K))
```

```python
import functools

import jax
import jax.numpy as jnp
from jax import lax
from jax.experimental import pallas as pl
from jax.experimental.pallas import tpu as pltpu
from jax.sharding import PartitionSpec as P

CHUNKS = 2
VMEM_BYTES = 48 * 1024 * 1024


def whole_vmem():
    return pl.BlockSpec(memory_space=pltpu.VMEM)


def gather_kernel(chunk, expo_count, listed_ref, samples_ref, out_ref, held):
    galaxy_count, rows, coeff_dim = held.shape
    sample_count = samples_ref.shape[0] // galaxy_count
    share = sample_count // expo_count
    part = share // CHUNKS
    group = 8
    out_row = lax.broadcasted_iota(jnp.int32, (group * rows, group * sample_count), 0)
    in_row = lax.broadcasted_iota(jnp.int32, (group * rows, group * sample_count), 1)
    within = out_row % rows
    wanted = (
        (out_row // rows) * sample_count
        + (within // part) * share
        + chunk * part
        + within % part
    )
    select = jnp.where(in_row == wanted, 1.0, 0.0).astype(jnp.bfloat16)
    for b in range(galaxy_count // group):
        block = samples_ref[b * group * sample_count : (b + 1) * group * sample_count, :]
        picked = jnp.dot(select, block, preferred_element_type=jnp.float32).astype(jnp.bfloat16)
        held[b * group : (b + 1) * group] = picked.reshape(group, rows, coeff_dim)

    @pl.loop(0, out_ref.shape[0], unroll=8)
    def _(slot):
        out_ref[slot] = held[jnp.maximum(listed_ref[slot], 0)]


def gather_slots(chunk, expo_count, listed, flat_samples, galaxy_count):
    rows = flat_samples.shape[0] // galaxy_count // CHUNKS
    coeff_dim = flat_samples.shape[1]
    return pl.pallas_call(
        functools.partial(gather_kernel, chunk, expo_count),
        out_shape=jax.ShapeDtypeStruct((listed.shape[0], rows, coeff_dim), jnp.bfloat16),
        in_specs=[pl.BlockSpec(memory_space=pltpu.SMEM), whole_vmem()],
        out_specs=whole_vmem(),
        scratch_shapes=[pltpu.VMEM((galaxy_count, rows, coeff_dim), jnp.bfloat16)],
        compiler_params=pltpu.CompilerParams(vmem_limit_bytes=VMEM_BYTES),
        cost_estimate=pl.CostEstimate(flops=10**8, bytes_accessed=3 * 10**6, transcendentals=0),
        name="gather_slots",
    )(listed, flat_samples)


def pair_kernel(inter_ref, incoming_ref, basis_ref, op_ref, cut_ref, weight_ref, grad_ref, like_ref, picked):
    tile = pl.program_id(0)
    cap, pixels = cut_ref.shape[1:]
    rows = incoming_ref.shape[1]

    @pl.when(tile == 0)
    def _():
        grad_ref[...] = jnp.zeros_like(grad_ref)

    for q in range(cap):
        picked[q * rows : (q + 1) * rows] = incoming_ref[jnp.maximum(inter_ref[tile, q], 0)]
    rendered = jnp.dot(picked[...], basis_ref[...], preferred_element_type=jnp.float32)
    rendered = rendered.astype(jnp.bfloat16)
    model = jnp.dot(rendered, op_ref[0], preferred_element_type=jnp.float32)
    resid = model.reshape(cap, rows, pixels) - cut_ref[0][:, None, :]
    weighted = weight_ref[0][:, None, :] * resid
    like_ref[0] = -0.5 / pixels * jnp.sum(weighted * resid, axis=-1)
    scaled = weighted.astype(jnp.bfloat16).reshape(cap * rows, pixels)
    last = (((1,), (1,)), ((), ()))
    backed = lax.dot_general(scaled, op_ref[0], last, preferred_element_type=jnp.float32)
    backed = backed.astype(jnp.bfloat16)
    grad = lax.dot_general(backed, basis_ref[...], last, preferred_element_type=jnp.float32)
    grad = (-1.0 / pixels * grad).astype(jnp.bfloat16)
    for q in range(cap):
        slot = inter_ref[tile, q]

        @pl.when(slot >= 0)
        def _():
            grad_ref[slot] = grad[q * rows : (q + 1) * rows]


def pair_terms(intersections, incoming, basis, operators, cutouts, pixel_weights):
    tiles, cap, pixels = cutouts.shape
    slots, rows, coeff_dim = incoming.shape
    flops = 4 * tiles * cap * rows * pixels * (pixels + coeff_dim)
    fixed = lambda t, inter: (0, 0, 0)
    moving = lambda t, inter: (t, 0, 0)
    return pl.pallas_call(
        pair_kernel,
        grid_spec=pltpu.PrefetchScalarGridSpec(
            num_scalar_prefetch=1,
            grid=(tiles,),
            in_specs=[
                pl.BlockSpec((slots, rows, coeff_dim), fixed),
                pl.BlockSpec((coeff_dim, pixels), lambda t, inter: (0, 0)),
                pl.BlockSpec((1, pixels, pixels), moving),
                pl.BlockSpec((1, cap, pixels), moving),
                pl.BlockSpec((1, cap, pixels), moving),
            ],
            out_specs=[
                pl.BlockSpec((slots, rows, coeff_dim), fixed),
                pl.BlockSpec((1, cap, rows), moving),
            ],
            scratch_shapes=[pltpu.VMEM((cap * rows, coeff_dim), jnp.bfloat16)],
        ),
        out_shape=[
            jax.ShapeDtypeStruct((slots, rows, coeff_dim), jnp.bfloat16),
            jax.ShapeDtypeStruct((tiles, cap, rows), jnp.float32),
        ],
        compiler_params=pltpu.CompilerParams(vmem_limit_bytes=VMEM_BYTES),
        cost_estimate=pl.CostEstimate(
            flops=flops, bytes_accessed=2 * operators.size + 4 * incoming.size, transcendentals=0
        ),
        name="pair_terms",
    )(intersections, incoming, basis, operators, cutouts, pixel_weights)


def sum_kernel(listed_ref, back_ref, out_ref, total):
    galaxy_count = total.shape[0] - 8
    expo_count = out_ref.shape[0]
    rows, coeff_dim = total.shape[1:]
    part = rows // expo_count
    total[...] = jnp.zeros_like(total)

    @pl.loop(0, back_ref.shape[0], unroll=8)
    def _(slot):
        listed = listed_ref[slot]
        place = jnp.where(listed >= 0, listed, galaxy_count)
        total[place] += back_ref[slot].astype(jnp.float32)

    for e in range(expo_count):
        mine = total[:galaxy_count, e * part : (e + 1) * part, :]
        out_ref[e] = mine.reshape(galaxy_count * part, coeff_dim)


def sum_galaxies(listed, back, galaxy_count, expo_count):
    slots, rows, coeff_dim = back.shape
    return pl.pallas_call(
        sum_kernel,
        out_shape=jax.ShapeDtypeStruct(
            (expo_count, galaxy_count * rows // expo_count, coeff_dim), jnp.float32
        ),
        in_specs=[pl.BlockSpec(memory_space=pltpu.SMEM), whole_vmem()],
        out_specs=whole_vmem(),
        scratch_shapes=[pltpu.VMEM((galaxy_count + 8, rows, coeff_dim), jnp.float32)],
        compiler_params=pltpu.CompilerParams(vmem_limit_bytes=VMEM_BYTES),
        cost_estimate=pl.CostEstimate(flops=10**6, bytes_accessed=3 * 10**6, transcendentals=0),
        name="sum_galaxies",
    )(listed, back)


def exact_dot(a, b):
    return jnp.dot(a, b, precision=lax.Precision.HIGHEST)


def per_device(samples, basis, operators, cutouts, pixel_weights, detections, intersections):
    galaxy_count, sample_count, coeff_dim = samples.shape
    sky_count, expo_count = lax.axis_size("sky"), lax.axis_size("expo")
    send_cap = detections.shape[3]
    slots = sky_count * send_cap
    part = sample_count // expo_count // CHUNKS
    listed = detections.reshape(slots)
    flat_samples = samples.reshape(galaxy_count * sample_count, coeff_dim)

    def swap(values, axis_name, count):
        shape = values.shape
        values = values.reshape(count, shape[0] // count, *shape[1:])
        values = lax.all_to_all(values, axis_name, split_axis=0, concat_axis=0, tiled=True)
        return values.reshape(shape)

    grads, likes = [], []
    for chunk in range(CHUNKS):
        outgoing = gather_slots(chunk, expo_count, listed, flat_samples, galaxy_count)
        incoming = swap(outgoing, "sky", sky_count)
        slot_grads, pair_like = pair_terms(
            intersections, incoming, basis, operators, cutouts, pixel_weights
        )
        back = swap(slot_grads, "sky", sky_count)
        summed = sum_galaxies(listed, back, galaxy_count, expo_count)
        summed = lax.psum_scatter(summed, "expo", scatter_dimension=0, tiled=True)
        grads.append(summed.reshape(galaxy_count, part, coeff_dim))
        likes.append(pair_like.reshape(-1, expo_count, part))

    pair_like = jnp.stack(likes, axis=2).reshape(-1, sample_count)
    holds = intersections.reshape(1, -1) == jnp.arange(slots, dtype=jnp.int32)[:, None]
    back_like = swap(exact_dot(holds.astype(jnp.float32), pair_like), "sky", sky_count)
    owns = listed[None, :] == jnp.arange(galaxy_count, dtype=jnp.int32)[:, None]
    like_part = exact_dot(owns.astype(jnp.float32), back_like)
    like_part = like_part.reshape(galaxy_count, expo_count, -1).transpose(1, 0, 2)
    like_out = jnp.sum(lax.all_to_all(like_part, "expo", split_axis=0, concat_axis=0), axis=0)
    return like_out, jnp.concatenate(grads, axis=1)


def solution(mesh):
    placed = (
        P("sky", None, None),
        P(),
        P(("expo", "sky"), None, None),
        P(("expo", "sky"), None, None),
        P(("expo", "sky"), None, None),
        P("expo", "sky", None, None),
        P(("expo", "sky"), None),
    )
    return jax.shard_map(
        per_device,
        mesh=mesh,
        in_specs=placed,
        out_specs=(P("sky", "expo"), P("sky", "expo", None)),
        check_vma=False,
    )
```

```python
import functools

import jax
import jax.numpy as jnp
from jax import lax
from jax.experimental import pallas as pl
from jax.experimental.pallas import tpu as pltpu
from jax.sharding import PartitionSpec as P

CHUNKS = 2
VMEM_BYTES = 48 * 1024 * 1024


def whole_vmem():
    return pl.BlockSpec(memory_space=pltpu.VMEM)


def gather_kernel(chunk, expo_count, listed_ref, samples_ref, out_ref, held):
    galaxy_count, rows, coeff_dim = held.shape
    sample_count = samples_ref.shape[0] // galaxy_count
    share = sample_count // expo_count
    part = share // CHUNKS
    group = 8
    out_row = lax.broadcasted_iota(jnp.int32, (group * rows, group * sample_count), 0)
    in_row = lax.broadcasted_iota(jnp.int32, (group * rows, group * sample_count), 1)
    within = out_row % rows
    wanted = (
        (out_row // rows) * sample_count
        + (within // part) * share
        + chunk * part
        + within % part
    )
    select = jnp.where(in_row == wanted, 1.0, 0.0).astype(jnp.bfloat16)
    for b in range(galaxy_count // group):
        block = samples_ref[b * group * sample_count : (b + 1) * group * sample_count, :]
        picked = jnp.dot(select, block, preferred_element_type=jnp.float32).astype(jnp.bfloat16)
        held[b * group : (b + 1) * group] = picked.reshape(group, rows, coeff_dim)

    @pl.loop(0, out_ref.shape[0], unroll=8)
    def _(slot):
        out_ref[slot] = held[jnp.maximum(listed_ref[slot], 0)]


def gather_slots(chunk, expo_count, listed, flat_samples, galaxy_count):
    rows = flat_samples.shape[0] // galaxy_count // CHUNKS
    coeff_dim = flat_samples.shape[1]
    return pl.pallas_call(
        functools.partial(gather_kernel, chunk, expo_count),
        out_shape=jax.ShapeDtypeStruct((listed.shape[0], rows, coeff_dim), jnp.bfloat16),
        in_specs=[pl.BlockSpec(memory_space=pltpu.SMEM), whole_vmem()],
        out_specs=whole_vmem(),
        scratch_shapes=[pltpu.VMEM((galaxy_count, rows, coeff_dim), jnp.bfloat16)],
        compiler_params=pltpu.CompilerParams(vmem_limit_bytes=VMEM_BYTES),
        cost_estimate=pl.CostEstimate(flops=10**8, bytes_accessed=3 * 10**6, transcendentals=0),
        name="gather_slots",
    )(listed, flat_samples)


def pair_kernel(inter_ref, incoming_ref, basis_ref, op_ref, cut_ref, weight_ref, grad_ref, like_ref, picked):
    tile = pl.program_id(0)
    cap, pixels = cut_ref.shape[1:]
    rows = incoming_ref.shape[1]

    @pl.when(tile == 0)
    def _():
        grad_ref[...] = jnp.zeros_like(grad_ref)

    for q in range(cap):
        picked[q * rows : (q + 1) * rows] = incoming_ref[jnp.maximum(inter_ref[tile, q], 0)]
    rendered = jnp.dot(picked[...], basis_ref[...], preferred_element_type=jnp.float32)
    rendered = rendered.astype(jnp.bfloat16)
    model = jnp.dot(rendered, op_ref[0], preferred_element_type=jnp.float32)
    resid = model.reshape(cap, rows, pixels) - cut_ref[0][:, None, :]
    weighted = weight_ref[0][:, None, :] * resid
    like_ref[0] = -0.5 / pixels * jnp.sum(weighted * resid, axis=-1)
    scaled = weighted.astype(jnp.bfloat16).reshape(cap * rows, pixels)
    last = (((1,), (1,)), ((), ()))
    backed = lax.dot_general(scaled, op_ref[0], last, preferred_element_type=jnp.float32)
    backed = backed.astype(jnp.bfloat16)
    grad = lax.dot_general(backed, basis_ref[...], last, preferred_element_type=jnp.float32)
    grad = (-1.0 / pixels * grad).astype(jnp.bfloat16)
    for q in range(cap):
        slot = inter_ref[tile, q]

        @pl.when(slot >= 0)
        def _():
            grad_ref[slot] = grad[q * rows : (q + 1) * rows]


def pair_terms(intersections, incoming, basis, operators, cutouts, pixel_weights):
    tiles, cap, pixels = cutouts.shape
    slots, rows, coeff_dim = incoming.shape
    flops = 4 * tiles * cap * rows * pixels * (pixels + coeff_dim)
    fixed = lambda t, inter: (0, 0, 0)
    moving = lambda t, inter: (t, 0, 0)
    return pl.pallas_call(
        pair_kernel,
        grid_spec=pltpu.PrefetchScalarGridSpec(
            num_scalar_prefetch=1,
            grid=(tiles,),
            in_specs=[
                pl.BlockSpec((slots, rows, coeff_dim), fixed),
                pl.BlockSpec((coeff_dim, pixels), lambda t, inter: (0, 0)),
                pl.BlockSpec((1, pixels, pixels), moving),
                pl.BlockSpec((1, cap, pixels), moving),
                pl.BlockSpec((1, cap, pixels), moving),
            ],
            out_specs=[
                pl.BlockSpec((slots, rows, coeff_dim), fixed),
                pl.BlockSpec((1, cap, rows), moving),
            ],
            scratch_shapes=[pltpu.VMEM((cap * rows, coeff_dim), jnp.bfloat16)],
        ),
        out_shape=[
            jax.ShapeDtypeStruct((slots, rows, coeff_dim), jnp.bfloat16),
            jax.ShapeDtypeStruct((tiles, cap, rows), jnp.float32),
        ],
        compiler_params=pltpu.CompilerParams(vmem_limit_bytes=VMEM_BYTES),
        cost_estimate=pl.CostEstimate(
            flops=flops, bytes_accessed=2 * operators.size + 4 * incoming.size, transcendentals=0
        ),
        name="pair_terms",
    )(intersections, incoming, basis, operators, cutouts, pixel_weights)


def sum_kernel(listed_ref, back_ref, out_ref, total):
    galaxy_count = total.shape[0] - 8
    expo_count = out_ref.shape[0]
    rows, coeff_dim = total.shape[1:]
    part = rows // expo_count
    total[...] = jnp.zeros_like(total)

    @pl.loop(0, back_ref.shape[0], unroll=8)
    def _(slot):
        listed = listed_ref[slot]
        place = jnp.where(listed >= 0, listed, galaxy_count)
        total[place] += back_ref[slot].astype(jnp.float32)

    for e in range(expo_count):
        mine = total[:galaxy_count, e * part : (e + 1) * part, :]
        out_ref[e] = mine.reshape(galaxy_count * part, coeff_dim).astype(out_ref.dtype)


def sum_galaxies(listed, back, galaxy_count, expo_count, kept):
    slots, rows, coeff_dim = back.shape
    return pl.pallas_call(
        sum_kernel,
        out_shape=jax.ShapeDtypeStruct(
            (expo_count, galaxy_count * rows // expo_count, coeff_dim), kept
        ),
        in_specs=[pl.BlockSpec(memory_space=pltpu.SMEM), whole_vmem()],
        out_specs=whole_vmem(),
        scratch_shapes=[pltpu.VMEM((galaxy_count + 8, rows, coeff_dim), jnp.float32)],
        compiler_params=pltpu.CompilerParams(vmem_limit_bytes=VMEM_BYTES),
        cost_estimate=pl.CostEstimate(flops=10**6, bytes_accessed=3 * 10**6, transcendentals=0),
        name="sum_galaxies",
    )(listed, back)


def exact_dot(a, b):
    return jnp.dot(a, b, precision=lax.Precision.HIGHEST)


def per_device(samples, basis, operators, cutouts, pixel_weights, detections, intersections):
    galaxy_count, sample_count, coeff_dim = samples.shape
    sky_count, expo_count = lax.axis_size("sky"), lax.axis_size("expo")
    send_cap = detections.shape[3]
    slots = sky_count * send_cap
    part = sample_count // expo_count // CHUNKS
    listed = detections.reshape(slots)
    flat_samples = samples.reshape(galaxy_count * sample_count, coeff_dim)

    def swap(values, axis_name, count):
        shape = values.shape
        values = values.reshape(count, shape[0] // count, *shape[1:])
        values = lax.all_to_all(values, axis_name, split_axis=0, concat_axis=0, tiled=True)
        return values.reshape(shape)

    incoming = []
    for chunk in range(CHUNKS):
        outgoing = gather_slots(chunk, expo_count, listed, flat_samples, galaxy_count)
        incoming.append(swap(outgoing, "sky", sky_count))
    slot_grads, likes, grads = [], [], []
    for chunk in range(CHUNKS):
        pair_grads, pair_like = pair_terms(
            intersections, incoming[chunk], basis, operators, cutouts, pixel_weights
        )
        if chunk + 1 < CHUNKS:
            pair_grads, incoming[chunk + 1] = lax.optimization_barrier(
                (pair_grads, incoming[chunk + 1])
            )
        slot_grads.append(pair_grads)
        likes.append(pair_like.reshape(-1, expo_count, part))
    for chunk in range(CHUNKS):
        back = swap(slot_grads[chunk], "sky", sky_count)
        last = chunk + 1 == CHUNKS
        if not last:
            back, slot_grads[chunk + 1] = lax.optimization_barrier((back, slot_grads[chunk + 1]))
        kept = jnp.bfloat16 if last else jnp.float32
        summed = sum_galaxies(listed, back, galaxy_count, expo_count, kept)
        if last:
            summed = lax.all_to_all(summed, "expo", split_axis=0, concat_axis=0, tiled=True)
            summed = jnp.sum(summed.astype(jnp.float32), axis=0)
        else:
            summed = lax.psum_scatter(summed, "expo", scatter_dimension=0, tiled=True)
        grads.append(summed.reshape(galaxy_count, part, coeff_dim))

    pair_like = jnp.stack(likes, axis=2).reshape(-1, sample_count)
    holds = intersections.reshape(1, -1) == jnp.arange(slots, dtype=jnp.int32)[:, None]
    back_like = swap(exact_dot(holds.astype(jnp.float32), pair_like), "sky", sky_count)
    owns = listed[None, :] == jnp.arange(galaxy_count, dtype=jnp.int32)[:, None]
    like_part = exact_dot(owns.astype(jnp.float32), back_like)
    like_part = like_part.reshape(galaxy_count, expo_count, -1).transpose(1, 0, 2)
    like_out = jnp.sum(lax.all_to_all(like_part, "expo", split_axis=0, concat_axis=0), axis=0)
    return like_out, jnp.concatenate(grads, axis=1)


def solution(mesh):
    placed = (
        P("sky", None, None),
        P(),
        P(("expo", "sky"), None, None),
        P(("expo", "sky"), None, None),
        P(("expo", "sky"), None, None),
        P("expo", "sky", None, None),
        P(("expo", "sky"), None),
    )
    return jax.shard_map(
        per_device,
        mesh=mesh,
        in_specs=placed,
        out_specs=(P("sky", "expo"), P("sky", "expo", None)),
        check_vma=False,
    )
```

```python
import functools

import jax
import jax.numpy as jnp
from jax import lax
from jax.experimental import pallas as pl
from jax.experimental.pallas import tpu as pltpu
from jax.sharding import PartitionSpec as P

CHUNKS = 2
VMEM_BYTES = 48 * 1024 * 1024
PAIR_VMEM_BYTES = 60 * 1024 * 1024


def whole_vmem():
    return pl.BlockSpec(memory_space=pltpu.VMEM)


def gather_kernel(chunk, expo_count, listed_ref, samples_ref, out_ref, held):
    galaxy_count, rows, coeff_dim = held.shape
    sample_count = samples_ref.shape[0] // galaxy_count
    share = sample_count // expo_count
    part = share // CHUNKS
    group = 8
    out_row = lax.broadcasted_iota(jnp.int32, (group * rows, group * sample_count), 0)
    in_row = lax.broadcasted_iota(jnp.int32, (group * rows, group * sample_count), 1)
    within = out_row % rows
    wanted = (
        (out_row // rows) * sample_count
        + (within // part) * share
        + chunk * part
        + within % part
    )
    select = jnp.where(in_row == wanted, 1.0, 0.0).astype(jnp.bfloat16)
    for b in range(galaxy_count // group):
        block = samples_ref[b * group * sample_count : (b + 1) * group * sample_count, :]
        picked = jnp.dot(select, block, preferred_element_type=jnp.float32).astype(jnp.bfloat16)
        held[b * group : (b + 1) * group] = picked.reshape(group, rows, coeff_dim)

    @pl.loop(0, out_ref.shape[0], unroll=8)
    def _(slot):
        out_ref[slot] = held[jnp.maximum(listed_ref[slot], 0)]


def gather_slots(chunk, expo_count, listed, flat_samples, galaxy_count):
    rows = flat_samples.shape[0] // galaxy_count // CHUNKS
    coeff_dim = flat_samples.shape[1]
    return pl.pallas_call(
        functools.partial(gather_kernel, chunk, expo_count),
        out_shape=jax.ShapeDtypeStruct((listed.shape[0], rows, coeff_dim), jnp.bfloat16),
        in_specs=[pl.BlockSpec(memory_space=pltpu.SMEM), whole_vmem()],
        out_specs=whole_vmem(),
        scratch_shapes=[pltpu.VMEM((galaxy_count, rows, coeff_dim), jnp.bfloat16)],
        compiler_params=pltpu.CompilerParams(vmem_limit_bytes=VMEM_BYTES),
        cost_estimate=pl.CostEstimate(flops=10**8, bytes_accessed=3 * 10**6, transcendentals=0),
        name="gather_slots",
    )(listed, flat_samples)


def pair_kernel(inter_ref, incoming_ref, basis_ref, op_ref, cut_ref, weight_ref, grad_ref, like_ref, picked):
    tile = pl.program_id(0)
    cap, pixels = cut_ref.shape[1:]
    rows = incoming_ref.shape[1]

    @pl.when(tile == 0)
    def _():
        grad_ref[...] = jnp.zeros_like(grad_ref)

    for q in range(cap):
        picked[q * rows : (q + 1) * rows] = incoming_ref[jnp.maximum(inter_ref[tile, q], 0)]
    rendered = jnp.dot(picked[...], basis_ref[...], preferred_element_type=jnp.float32)
    rendered = rendered.astype(jnp.bfloat16)
    model = jnp.dot(rendered, op_ref[0], preferred_element_type=jnp.float32)
    resid = model.reshape(cap, rows, pixels) - cut_ref[0][:, None, :]
    weighted = weight_ref[0][:, None, :] * resid
    like_ref[0] = -0.5 / pixels * jnp.sum(weighted * resid, axis=-1)
    scaled = weighted.astype(jnp.bfloat16).reshape(cap * rows, pixels)
    last = (((1,), (1,)), ((), ()))
    backed = lax.dot_general(scaled, op_ref[0], last, preferred_element_type=jnp.float32)
    backed = backed.astype(jnp.bfloat16)
    grad = lax.dot_general(backed, basis_ref[...], last, preferred_element_type=jnp.float32)
    grad = (-1.0 / pixels * grad).astype(jnp.bfloat16)
    for q in range(cap):
        slot = inter_ref[tile, q]

        @pl.when(slot >= 0)
        def _():
            grad_ref[slot] = grad[q * rows : (q + 1) * rows]


def pair_terms(intersections, incoming, basis, operators, cutouts, pixel_weights):
    tiles, cap, pixels = cutouts.shape
    slots, rows, coeff_dim = incoming.shape
    flops = 4 * tiles * cap * rows * pixels * (pixels + coeff_dim)
    fixed = lambda t, inter: (0, 0, 0)
    moving = lambda t, inter: (t, 0, 0)
    return pl.pallas_call(
        pair_kernel,
        grid_spec=pltpu.PrefetchScalarGridSpec(
            num_scalar_prefetch=1,
            grid=(tiles,),
            in_specs=[
                pl.BlockSpec((slots, rows, coeff_dim), fixed),
                pl.BlockSpec((coeff_dim, pixels), lambda t, inter: (0, 0)),
                pl.BlockSpec((1, pixels, pixels), moving),
                pl.BlockSpec((1, cap, pixels), moving),
                pl.BlockSpec((1, cap, pixels), moving),
            ],
            out_specs=[
                pl.BlockSpec((slots, rows, coeff_dim), fixed),
                pl.BlockSpec((1, cap, rows), moving),
            ],
            scratch_shapes=[pltpu.VMEM((cap * rows, coeff_dim), jnp.bfloat16)],
        ),
        out_shape=[
            jax.ShapeDtypeStruct((slots, rows, coeff_dim), jnp.bfloat16),
            jax.ShapeDtypeStruct((tiles, cap, rows), jnp.float32),
        ],
        compiler_params=pltpu.CompilerParams(vmem_limit_bytes=PAIR_VMEM_BYTES),
        cost_estimate=pl.CostEstimate(
            flops=flops, bytes_accessed=2 * operators.size + 4 * incoming.size, transcendentals=0
        ),
        name="pair_terms",
    )(intersections, incoming, basis, operators, cutouts, pixel_weights)


def sum_kernel(listed_ref, back_ref, *refs):
    *extra, out_ref, total = refs
    galaxy_count = total.shape[0] - 8
    expo_count = out_ref.shape[0]
    rows, coeff_dim = total.shape[1:]
    part = rows // expo_count
    total[...] = jnp.zeros_like(total)

    @pl.loop(0, back_ref.shape[0], unroll=8)
    def _(slot):
        listed = listed_ref[slot]
        place = jnp.where(listed >= 0, listed, galaxy_count)
        total[place] += back_ref[slot].astype(jnp.float32)

    for e in range(expo_count):
        mine = total[:galaxy_count, e * part : (e + 1) * part, :]
        grad_rows = galaxy_count * part
        out_ref[e, :grad_rows] = mine.reshape(grad_rows, coeff_dim).astype(out_ref.dtype)
        for extra_ref in extra:
            out_ref[e, grad_rows:] = extra_ref[e]


def sum_galaxies(listed, back, galaxy_count, expo_count, kept, extra=()):
    slots, rows, coeff_dim = back.shape
    out_rows = galaxy_count * rows // expo_count + sum(one.shape[1] for one in extra)
    return pl.pallas_call(
        sum_kernel,
        out_shape=jax.ShapeDtypeStruct((expo_count, out_rows, coeff_dim), kept),
        in_specs=[pl.BlockSpec(memory_space=pltpu.SMEM)] + [whole_vmem()] * (1 + len(extra)),
        out_specs=whole_vmem(),
        scratch_shapes=[pltpu.VMEM((galaxy_count + 8, rows, coeff_dim), jnp.float32)],
        compiler_params=pltpu.CompilerParams(vmem_limit_bytes=VMEM_BYTES),
        cost_estimate=pl.CostEstimate(flops=10**6, bytes_accessed=3 * 10**6, transcendentals=0),
        name="sum_galaxies",
    )(listed, back, *extra)


def three_terms(values):
    terms = []
    for _ in range(3):
        term = lax.reduce_precision(values, exponent_bits=8, mantissa_bits=7)
        terms.append(term.astype(jnp.bfloat16))
        values = values - term
    return jnp.stack(terms)


def exact_dot(a, b):
    return jnp.dot(a, b, precision=lax.Precision.HIGHEST)


def per_device(samples, basis, operators, cutouts, pixel_weights, detections, intersections):
    galaxy_count, sample_count, coeff_dim = samples.shape
    sky_count, expo_count = lax.axis_size("sky"), lax.axis_size("expo")
    send_cap = detections.shape[3]
    slots = sky_count * send_cap
    part = sample_count // expo_count // CHUNKS
    listed = detections.reshape(slots)
    flat_samples = samples.reshape(galaxy_count * sample_count, coeff_dim)

    def swap(values, axis_name, count):
        shape = values.shape
        values = values.reshape(count, shape[0] // count, *shape[1:])
        values = lax.all_to_all(values, axis_name, split_axis=0, concat_axis=0, tiled=True)
        return values.reshape(shape)

    incoming = []
    for chunk in range(CHUNKS):
        outgoing = gather_slots(chunk, expo_count, listed, flat_samples, galaxy_count)
        incoming.append(swap(outgoing, "sky", sky_count))
    slot_grads, likes, grads = [], [], []
    for chunk in range(CHUNKS):
        pair_grads, pair_like = pair_terms(
            intersections, incoming[chunk], basis, operators, cutouts, pixel_weights
        )
        if chunk + 1 < CHUNKS:
            pair_grads, incoming[chunk + 1] = lax.optimization_barrier(
                (pair_grads, incoming[chunk + 1])
            )
        slot_grads.append(pair_grads)
        likes.append(pair_like.reshape(-1, expo_count, part))

    share = sample_count // expo_count
    pair_like = jnp.stack(likes, axis=2).reshape(-1, sample_count)
    holds = intersections.reshape(1, -1) == jnp.arange(slots, dtype=jnp.int32)[:, None]
    slot_like = exact_dot(holds.astype(jnp.float32), pair_like)
    slot_like = slot_like.reshape(sky_count, send_cap * sample_count)
    every_like = lax.all_gather(slot_like, "sky")
    back_like = lax.dynamic_index_in_dim(every_like, lax.axis_index("sky"), 1, keepdims=False)
    owns = listed[None, :] == jnp.arange(galaxy_count, dtype=jnp.int32)[:, None]
    like_part = exact_dot(owns.astype(jnp.float32), back_like.reshape(slots, sample_count))
    like_part = like_part.reshape(galaxy_count, expo_count, share).transpose(1, 0, 2)
    packed = jnp.moveaxis(three_terms(like_part), 0, 1).reshape(expo_count, -1)
    like_rows = -(-packed.shape[1] // (16 * coeff_dim)) * 16
    used = packed.shape[1]
    packed = jnp.pad(packed, ((0, 0), (0, like_rows * coeff_dim - used)))
    packed = packed.reshape(expo_count, like_rows, coeff_dim)

    for chunk in range(CHUNKS):
        back = swap(slot_grads[chunk], "sky", sky_count)
        if chunk + 1 < CHUNKS:
            back, slot_grads[chunk + 1] = lax.optimization_barrier((back, slot_grads[chunk + 1]))
            summed = sum_galaxies(listed, back, galaxy_count, expo_count, jnp.float32)
            summed = lax.psum_scatter(summed, "expo", scatter_dimension=0, tiled=True)
            grads.append(summed.reshape(galaxy_count, part, coeff_dim))
        else:
            summed = sum_galaxies(listed, back, galaxy_count, expo_count, jnp.bfloat16, (packed,))
            summed = lax.all_to_all(summed, "expo", split_axis=0, concat_axis=0, tiled=True)
            summed = summed.astype(jnp.float32)
            mine = jnp.sum(summed[:, : galaxy_count * part], axis=0)
            grads.append(mine.reshape(galaxy_count, part, coeff_dim))
            terms = summed[:, galaxy_count * part :].reshape(expo_count, -1)[:, :used]
            like_out = jnp.sum(terms.reshape(expo_count * 3, galaxy_count, share), axis=0)
    return like_out, jnp.concatenate(grads, axis=1)


def solution(mesh):
    placed = (
        P("sky", None, None),
        P(),
        P(("expo", "sky"), None, None),
        P(("expo", "sky"), None, None),
        P(("expo", "sky"), None, None),
        P("expo", "sky", None, None),
        P(("expo", "sky"), None),
    )
    return jax.shard_map(
        per_device,
        mesh=mesh,
        in_specs=placed,
        out_specs=(P("sky", "expo"), P("sky", "expo", None)),
        check_vma=False,
    )
```

```python
import functools

import jax
import jax.numpy as jnp
from jax import lax
from jax.experimental import pallas as pl
from jax.experimental.pallas import tpu as pltpu
from jax.sharding import PartitionSpec as P

CHUNKS = 2
VMEM_BYTES = 48 * 1024 * 1024
PAIR_VMEM_BYTES = 60 * 1024 * 1024


def whole_vmem():
    return pl.BlockSpec(memory_space=pltpu.VMEM)


def gather_kernel(chunk, expo_count, listed_ref, samples_ref, out_ref, held):
    galaxy_count, rows, coeff_dim = held.shape
    sample_count = samples_ref.shape[0] // galaxy_count
    share = sample_count // expo_count
    part = share // CHUNKS
    group = 8
    out_row = lax.broadcasted_iota(jnp.int32, (group * rows, group * sample_count), 0)
    in_row = lax.broadcasted_iota(jnp.int32, (group * rows, group * sample_count), 1)
    within = out_row % rows
    wanted = (
        (out_row // rows) * sample_count
        + (within // part) * share
        + chunk * part
        + within % part
    )
    select = jnp.where(in_row == wanted, 1.0, 0.0).astype(jnp.bfloat16)
    for b in range(galaxy_count // group):
        block = samples_ref[b * group * sample_count : (b + 1) * group * sample_count, :]
        picked = jnp.dot(select, block, preferred_element_type=jnp.float32).astype(jnp.bfloat16)
        held[b * group : (b + 1) * group] = picked.reshape(group, rows, coeff_dim)

    @pl.loop(0, out_ref.shape[0], unroll=8)
    def _(slot):
        out_ref[slot] = held[jnp.maximum(listed_ref[slot], 0)]


def gather_slots(chunk, expo_count, listed, flat_samples, galaxy_count):
    rows = flat_samples.shape[0] // galaxy_count // CHUNKS
    coeff_dim = flat_samples.shape[1]
    return pl.pallas_call(
        functools.partial(gather_kernel, chunk, expo_count),
        out_shape=jax.ShapeDtypeStruct((listed.shape[0], rows, coeff_dim), jnp.bfloat16),
        in_specs=[pl.BlockSpec(memory_space=pltpu.SMEM), whole_vmem()],
        out_specs=whole_vmem(),
        scratch_shapes=[pltpu.VMEM((galaxy_count, rows, coeff_dim), jnp.bfloat16)],
        compiler_params=pltpu.CompilerParams(vmem_limit_bytes=VMEM_BYTES),
        cost_estimate=pl.CostEstimate(flops=10**8, bytes_accessed=3 * 10**6, transcendentals=0),
        name="gather_slots",
    )(listed, flat_samples)


def pair_kernel(inter_ref, incoming_ref, basis_ref, op_ref, cut_ref, weight_ref, grad_ref, like_ref, picked):
    tile = pl.program_id(0)
    cap, pixels = cut_ref.shape[1:]
    rows = incoming_ref.shape[1]

    @pl.when(tile == 0)
    def _():
        grad_ref[...] = jnp.zeros_like(grad_ref)

    for q in range(cap):
        picked[q * rows : (q + 1) * rows] = incoming_ref[jnp.maximum(inter_ref[tile, q], 0)]
    rendered = jnp.dot(picked[...], basis_ref[...], preferred_element_type=jnp.float32)
    rendered = rendered.astype(jnp.bfloat16)
    model = jnp.dot(rendered, op_ref[0], preferred_element_type=jnp.float32)
    resid = model.reshape(cap, rows, pixels) - cut_ref[0][:, None, :]
    weighted = weight_ref[0][:, None, :] * resid
    like_ref[0] = -0.5 / pixels * jnp.sum(weighted * resid, axis=-1)
    scaled = weighted.astype(jnp.bfloat16).reshape(cap * rows, pixels)
    last = (((1,), (1,)), ((), ()))
    backed = lax.dot_general(scaled, op_ref[0], last, preferred_element_type=jnp.float32)
    backed = backed.astype(jnp.bfloat16)
    grad = lax.dot_general(backed, basis_ref[...], last, preferred_element_type=jnp.float32)
    grad = (-1.0 / pixels * grad).astype(jnp.bfloat16)
    for q in range(cap):
        slot = inter_ref[tile, q]

        @pl.when(slot >= 0)
        def _():
            grad_ref[slot] = grad[q * rows : (q + 1) * rows]


def pair_terms(intersections, incoming, basis, operators, cutouts, pixel_weights):
    tiles, cap, pixels = cutouts.shape
    slots, rows, coeff_dim = incoming.shape
    flops = 4 * tiles * cap * rows * pixels * (pixels + coeff_dim)
    fixed = lambda t, inter: (0, 0, 0)
    moving = lambda t, inter: (t, 0, 0)
    return pl.pallas_call(
        pair_kernel,
        grid_spec=pltpu.PrefetchScalarGridSpec(
            num_scalar_prefetch=1,
            grid=(tiles,),
            in_specs=[
                pl.BlockSpec((slots, rows, coeff_dim), fixed),
                pl.BlockSpec((coeff_dim, pixels), lambda t, inter: (0, 0)),
                pl.BlockSpec((1, pixels, pixels), moving),
                pl.BlockSpec((1, cap, pixels), moving),
                pl.BlockSpec((1, cap, pixels), moving),
            ],
            out_specs=[
                pl.BlockSpec((slots, rows, coeff_dim), fixed),
                pl.BlockSpec((1, cap, rows), moving),
            ],
            scratch_shapes=[pltpu.VMEM((cap * rows, coeff_dim), jnp.bfloat16)],
        ),
        out_shape=[
            jax.ShapeDtypeStruct((slots, rows, coeff_dim), jnp.bfloat16),
            jax.ShapeDtypeStruct((tiles, cap, rows), jnp.float32),
        ],
        compiler_params=pltpu.CompilerParams(vmem_limit_bytes=PAIR_VMEM_BYTES),
        cost_estimate=pl.CostEstimate(
            flops=flops, bytes_accessed=2 * operators.size + 4 * incoming.size, transcendentals=0
        ),
        name="pair_terms",
    )(intersections, incoming, basis, operators, cutouts, pixel_weights)


def sum_kernel(listed_ref, back_ref, *refs):
    *extra, out_ref, total = refs
    galaxy_count = total.shape[0] - 8
    expo_count = out_ref.shape[0]
    rows, coeff_dim = total.shape[1:]
    part = rows // expo_count
    total[...] = jnp.zeros_like(total)

    @pl.loop(0, back_ref.shape[0], unroll=8)
    def _(slot):
        listed = listed_ref[slot]
        place = jnp.where(listed >= 0, listed, galaxy_count)
        total[place] += back_ref[slot].astype(jnp.float32)

    for e in range(expo_count):
        mine = total[:galaxy_count, e * part : (e + 1) * part, :]
        grad_rows = galaxy_count * part
        out_ref[e, :grad_rows] = mine.reshape(grad_rows, coeff_dim).astype(out_ref.dtype)
        for extra_ref in extra:
            out_ref[e, grad_rows:] = extra_ref[e]


def sum_galaxies(listed, back, galaxy_count, expo_count, kept, extra=()):
    slots, rows, coeff_dim = back.shape
    out_rows = galaxy_count * rows // expo_count + sum(one.shape[1] for one in extra)
    return pl.pallas_call(
        sum_kernel,
        out_shape=jax.ShapeDtypeStruct((expo_count, out_rows, coeff_dim), kept),
        in_specs=[pl.BlockSpec(memory_space=pltpu.SMEM)] + [whole_vmem()] * (1 + len(extra)),
        out_specs=whole_vmem(),
        scratch_shapes=[pltpu.VMEM((galaxy_count + 8, rows, coeff_dim), jnp.float32)],
        compiler_params=pltpu.CompilerParams(vmem_limit_bytes=VMEM_BYTES),
        cost_estimate=pl.CostEstimate(flops=10**6, bytes_accessed=3 * 10**6, transcendentals=0),
        name="sum_galaxies",
    )(listed, back, *extra)


def three_terms(values):
    terms = []
    for _ in range(3):
        term = lax.reduce_precision(values, exponent_bits=8, mantissa_bits=7)
        terms.append(term.astype(jnp.bfloat16))
        values = values - term
    return jnp.stack(terms)


def exact_dot(a, b):
    return jnp.dot(a, b, precision=lax.Precision.HIGHEST)


def per_device(samples, basis, operators, cutouts, pixel_weights, detections, intersections):
    galaxy_count, sample_count, coeff_dim = samples.shape
    sky_count, expo_count = lax.axis_size("sky"), lax.axis_size("expo")
    send_cap = detections.shape[3]
    slots = sky_count * send_cap
    part = sample_count // expo_count // CHUNKS
    listed = detections.reshape(slots)
    flat_samples = samples.reshape(galaxy_count * sample_count, coeff_dim)

    def swap(values, axis_name, count):
        shape = values.shape
        values = values.reshape(count, shape[0] // count, *shape[1:])
        values = lax.all_to_all(values, axis_name, split_axis=0, concat_axis=0, tiled=True)
        return values.reshape(shape)

    incoming = []
    for chunk in range(CHUNKS):
        outgoing = gather_slots(chunk, expo_count, listed, flat_samples, galaxy_count)
        incoming.append(swap(outgoing, "sky", sky_count))
    slot_grads, likes, grads = [], [], []
    for chunk in range(CHUNKS):
        pair_grads, pair_like = pair_terms(
            intersections, incoming[chunk], basis, operators, cutouts, pixel_weights
        )
        if chunk + 1 < CHUNKS:
            pair_grads, incoming[chunk + 1] = lax.optimization_barrier(
                (pair_grads, incoming[chunk + 1])
            )
        slot_grads.append(pair_grads)
        likes.append(pair_like.reshape(-1, expo_count, part))

    share = sample_count // expo_count
    pair_like = jnp.stack(likes, axis=2).reshape(-1, sample_count)
    holds = intersections.reshape(1, -1) == jnp.arange(slots, dtype=jnp.int32)[:, None]
    slot_like = exact_dot(holds.astype(jnp.float32), pair_like)
    slot_like = slot_like.reshape(sky_count, send_cap * sample_count)
    me = lax.axis_index("sky")
    back_like = jnp.zeros_like(slot_like)
    for shift in range(sky_count):
        row = lax.dynamic_index_in_dim(slot_like, (me + shift) % sky_count, 0)
        if shift:
            pairs = [(c, (c + shift) % sky_count) for c in range(sky_count)]
            row = lax.ppermute(row, "sky", pairs)
        source = (me + sky_count - shift) % sky_count
        back_like = lax.dynamic_update_index_in_dim(back_like, row, source, 0)
    owns = listed[None, :] == jnp.arange(galaxy_count, dtype=jnp.int32)[:, None]
    like_part = exact_dot(owns.astype(jnp.float32), back_like.reshape(slots, sample_count))
    like_part = like_part.reshape(galaxy_count, expo_count, share).transpose(1, 0, 2)
    packed = jnp.moveaxis(three_terms(like_part), 0, 1).reshape(expo_count, -1)
    like_rows = -(-packed.shape[1] // (16 * coeff_dim)) * 16
    used = packed.shape[1]
    packed = jnp.pad(packed, ((0, 0), (0, like_rows * coeff_dim - used)))
    packed = packed.reshape(expo_count, like_rows, coeff_dim)

    for chunk in range(CHUNKS):
        back = swap(slot_grads[chunk], "sky", sky_count)
        if chunk + 1 < CHUNKS:
            back, slot_grads[chunk + 1] = lax.optimization_barrier((back, slot_grads[chunk + 1]))
            summed = sum_galaxies(listed, back, galaxy_count, expo_count, jnp.float32)
            summed = lax.psum_scatter(summed, "expo", scatter_dimension=0, tiled=True)
            grads.append(summed.reshape(galaxy_count, part, coeff_dim))
        else:
            summed = sum_galaxies(listed, back, galaxy_count, expo_count, jnp.bfloat16, (packed,))
            summed = lax.all_to_all(summed, "expo", split_axis=0, concat_axis=0, tiled=True)
            summed = summed.astype(jnp.float32)
            mine = jnp.sum(summed[:, : galaxy_count * part], axis=0)
            grads.append(mine.reshape(galaxy_count, part, coeff_dim))
            terms = summed[:, galaxy_count * part :].reshape(expo_count, -1)[:, :used]
            like_out = jnp.sum(terms.reshape(expo_count * 3, galaxy_count, share), axis=0)
    return like_out, jnp.concatenate(grads, axis=1)


def solution(mesh):
    placed = (
        P("sky", None, None),
        P(),
        P(("expo", "sky"), None, None),
        P(("expo", "sky"), None, None),
        P(("expo", "sky"), None, None),
        P("expo", "sky", None, None),
        P(("expo", "sky"), None),
    )
    return jax.shard_map(
        per_device,
        mesh=mesh,
        in_specs=placed,
        out_specs=(P("sky", "expo"), P("sky", "expo", None)),
        check_vma=False,
    )
```
